32 devices in a mesh: groups: 2 (over y), expert: 4 (over z), tensor: 4 (over x, core).
Axes of the slice: x: 2, y: 2, z: 4, core: 2. Of those that a mesh axis runs over, the one named last changes fastest.
Arguments:
- source_states: bfloat16 [2048, 2048], P(('groups', 'expert')), parts along dimension 0, may hold values from -6 to 6
- routes: int32 [2048, 2], P(('groups', 'expert')), parts along dimension 0, may hold values from 0 to 3, all different within a row; in each aligned block of 256 rows (0 to 255, 256 to 511, ...) at most 256 rows name the same one
- router_weight: bfloat16 [2048, 4], replicated, may hold values from -0.125 to 0.125
- fc1_weight: bfloat16 [4, 2048, 8192], P('expert', None, 'tensor'), may hold values from -0.125 to 0.125
- fc2_weight: bfloat16 [4, 8192, 2048], P('expert', 'tensor'), may hold values from -0.09375 to 0.09375
- lengths: int32 [8, 8], P(('groups', 'expert')), parts along dimension 0, may hold values from 1 to 48, 256 in all within a row
- lang_ids: int32 [64, 6], P(('groups', 'expert')), parts along dimension 0, may hold values from 0 to 5, each once within a row
- pivot_states: bfloat16 [6, 2048], replicated, may hold values from -480 to 480
- query_weight: bfloat16 [2048, 2048], P(None, 'tensor'), may hold values from -0.125 to 0.125
- key_weight: bfloat16 [2048, 2048], P(None, 'tensor'), may hold values from -0.125 to 0.125
- value_weight: bfloat16 [2048, 2048], P(None, 'tensor'), may hold values from -0.125 to 0.125
- out_weight: bfloat16 [2048, 2048], P('tensor'), may hold values from -0.125 to 0.125
Outputs:
- encoded_states: bfloat16 [2048, 2048], P(('groups', 'expert'), 'tensor'), parts along dimension 0
- decoder_states: bfloat16 [384, 2048], P(('groups', 'expert')), parts along dimension 0
The draws below stay inside these ranges and needn't reach their ends.
There are 2 independent parts, one for each index of `groups`. The reference program is written for one: setup_inputs(seed, part) draws one part's arguments, and reference() takes and returns one part's arrays. A program takes and returns all parts, laid end to end along the dimension named above; an argument that names none is the same for every part. Nothing has to cross between parts.
Inputs may be any that keep to these rules, and one draw needn't show every extreme that they name: `routes`: each token names two different experts; among the 256 tokens of one block no expert is named more than 256 times. `lengths`: each row sums to 256. `lang_ids`: each row names every pivot language once.
All inputs are finite; a program needn't handle non-finite values.
Results may differ from the reference program's by a relative error of at most 0.012.
Values may be sent and summed in bfloat16 or wider, within the bound.
A program may use at most 128 MiB of HBM per device.

```python
import math
import jax
import jax.numpy as jnp
import numpy as np
from jax import lax

D = 2048
FF = 8192
HEADS = 16
HD = 128
TOK_DEV = 256
QRY = 8
LMAX = 48
PIVOTS = 6
EXPERTS = 4
QBLOCKS = 4
SLICES = 4
CAP = 256
TOKENS = 1024
QUERIES = 32
ROWS = 192


def draw_pivot_states(key, part):
    values = jnp.clip(jax.random.normal(key, (PIVOTS, D), jnp.float32), -4.0, 4.0)
    return values.astype(jnp.bfloat16)


def spiked(result, own_key, source, target, shards_of, factor):
    def block_of(position):
        return (jnp.arange(result.shape[position]) // (result.shape[position] // shards_of)).reshape((-1,) + (1,) * (result.ndim - 1 - position))

    one_side = jax.random.permutation(own_key, shards_of)[block_of(target)]
    other_side = (block_of(target) + shards_of // 2) % shards_of
    return jnp.where((block_of(source) == one_side) | (block_of(source) == other_side), factor * result, result)


def shard_levels(rng, shape, split, low, top_value):
    def one(position, shards_of):
        heights = jax.random.uniform(jax.random.fold_in(jax.random.fold_in(rng, 6), position), (shards_of,), jnp.float32, low / len(split), top_value / len(split))
        return jnp.repeat(jnp.exp(heights), shape[position] // shards_of).reshape((-1,) + (1,) * (len(shape) - position - 1))

    level = one(*split[0])
    for cut in split[1:]:
        level = level * one(*cut)
    return level


def profile(number_of, total, most, skew):
    loads = [(1 << 20) // math.isqrt(grade ** skew) + 1 for grade in range(2, number_of + 1)]
    surplus, counts = total - most - (number_of - 1), [1] * (number_of - 1)
    while surplus > 0:
        candidates = [i for i in range(number_of - 1) if counts[i] < most]
        pool, budget = sum([loads[i] for i in candidates]), surplus
        for i in candidates:
            addition = min(most - counts[i], max(1, budget * loads[i] // pool), surplus)
            counts[i] = counts[i] + addition
            surplus = surplus - addition
    return np.array([most] + counts)


def uneven(key, amount, total, reach, lean):
    if amount == 2:
        one = jax.random.randint(key, (), max(1, total - reach), min(reach, total - 1) + 1)
        return jnp.stack([one, total - one])
    sizes = jnp.asarray(profile(amount, total, reach, lean), jnp.int32)
    pairs = (amount - 1) // 2
    donor, sink = sizes[1:1 + 2 * pairs:2], sizes[2:2 + 2 * pairs:2]
    margin = jnp.minimum(donor - 1, reach - sink)
    passed = jax.random.randint(jax.random.fold_in(key, 1), (pairs,), 0, 1 << 20) % (margin + 1)
    sizes = sizes.at[1:1 + 2 * pairs:2].set(donor - passed).at[2:2 + 2 * pairs:2].set(sink + passed)
    return sizes[jax.random.permutation(jax.random.fold_in(key, 2), amount)]


def routed_block(stream_key, own, number, rows, number_of, top, reach, lean):
    sequence = jax.random.permutation(stream_key, number_of)
    crowded, ordinary = shares(number_of, rows * top, reach, lean, True), shares(number_of, rows * top, reach, lean, False)
    places = jnp.arange(number_of)

    def named(sizes, rotation):
        used = int((sizes > 0).sum())
        fixed = max(1, used // 4)
        passed = fixed + (places - fixed + rotation * (used - fixed)) % max(1, number_of - fixed)
        return jnp.zeros((number_of,), jnp.int32).at[sequence[jnp.where(places < fixed, places, passed)]].set(jnp.asarray(sizes, jnp.int32))

    sizes = jnp.where(number % 4 == 0, named(crowded, number // 4), named(ordinary, number - number // 4 - 1))
    mixed = jax.random.permutation(jax.random.fold_in(own, 3), number_of)
    donor, taker = mixed[0:number_of // 2 * 2:2], mixed[1:number_of // 2 * 2:2]
    margin = jnp.minimum(sizes[donor] - 1, reach - sizes[taker]) // 2
    margin = jnp.where((donor == sequence[0]) | (taker == sequence[0]) | (sizes[taker] == 0), 0, jnp.maximum(margin, 0))
    passed = jax.random.randint(jax.random.fold_in(own, 4), (number_of // 2,), 0, 1 << 20) % (margin + 1)
    sizes = sizes.at[donor].add(-passed).at[taker].add(passed)
    labels = jnp.searchsorted(jnp.cumsum(sizes), jnp.arange(rows * top), side="right").astype(jnp.int32)
    grid = labels.reshape(top, rows).T
    grid = grid[jax.random.permutation(jax.random.fold_in(own, 1), rows)]
    rotation = jax.random.randint(jax.random.fold_in(own, 2), (rows, 1), 0, top)
    return jnp.take_along_axis(grid, (jnp.arange(top)[None, :] + rotation) % top, axis=1)


def shares(count, total, bound, slope, full):
    portions = [(1 << 20) // math.isqrt(standing ** slope) + 1 for standing in range(1, count + 1)]
    largest = bound if full else min(bound, max(-(-total // count), total * portions[0] // sum(portions)))
    least = 1 if total - largest >= count - 1 else 0
    given, spare = [largest] + [least] * (count - 1), total - largest - least * (count - 1)
    while spare > 0:
        free = [i for i in range(1, count) if given[i] < largest] or [i for i in range(1, count) if given[i] < bound]
        pool, left = sum([portions[i] for i in free]), spare
        for i in free:
            extra = min(bound - given[i], max(1, left * portions[i] // pool), spare)
            given[i] = given[i] + extra
            spare = spare - extra
    return np.array(given)


def gaussian(stream_key, shape, deviation, most, split=(), kind=jnp.bfloat16):
    entries = jax.random.normal(stream_key, shape, jnp.float32) * deviation
    if len(split) > 0:
        entries = shard_levels(stream_key, shape, split, -0.22, 0.18) * entries
    return jnp.clip(entries, min=-most, max=most).astype(kind)


def heavy_noise(own_key, extent, scale, bound, shards, heavy, kind=jnp.bfloat16):
    result = scale * jax.random.normal(own_key, extent, jnp.float32)
    if shards:
        result = result * shard_levels(own_key, extent, shards, -0.22, 0.18)
    return jnp.clip(spiked(result, jax.random.fold_in(own_key, 3), *heavy), -bound, bound).astype(kind)


def setup_inputs(seed: int = 0, part: int = 0) -> dict:
    arg_keys = jax.random.split(jax.random.key(seed), 13)
    own_keys = jax.random.split(jax.random.fold_in(arg_keys[12], part), 13)
    source_states = gaussian(own_keys[0], (TOKENS, D), 1.0, 6.0, ((0, 4),))
    routes_keys = jax.random.split(jax.random.fold_in(own_keys[1], 1), TOKENS // TOK_DEV)
    routes_turns = jax.random.permutation(jax.random.fold_in(own_keys[1], 3), TOKENS // TOK_DEV)
    routes = jax.vmap(lambda own, number: routed_block(jax.random.fold_in(own_keys[1], 2), own, number, TOK_DEV, EXPERTS, 2, CAP, 1))(routes_keys, routes_turns).reshape((TOKENS, 2))
    router_weight = gaussian(arg_keys[2], (D, EXPERTS), D ** -0.5, 0.125)
    fc1_weight = gaussian(arg_keys[3], (EXPERTS, D, FF), D ** -0.5, 0.125, ((0, 4), (2, 4)))
    fc2_weight = heavy_noise(arg_keys[4], (EXPERTS, FF, D), FF ** -0.5, 0.09375, ((0, 4), (1, 4)), (1, 2, 4, 2.0))
    lengths = jax.vmap(lambda own: uneven(own, QRY, TOK_DEV, LMAX, 2))(jax.random.split(own_keys[5], QBLOCKS)).reshape((QBLOCKS, QRY)).astype(jnp.int32)
    lang_ids = jax.vmap(lambda own: jax.random.permutation(own, PIVOTS))(jax.random.split(own_keys[6], QUERIES)).reshape((QUERIES, PIVOTS)).astype(jnp.int32)
    pivot_states = draw_pivot_states(jax.random.fold_in(arg_keys[12], 71), part)
    query_weight = gaussian(arg_keys[8], (D, D), D ** -0.5, 0.125, ((1, 4),))
    key_weight = gaussian(arg_keys[9], (D, D), D ** -0.5, 0.125, ((1, 4),))
    value_weight = gaussian(arg_keys[10], (D, D), D ** -0.5, 0.125, ((1, 4),))
    out_weight = gaussian(arg_keys[11], (D, D), D ** -0.5, 0.125, ((0, 4),))
    return {"source_states": source_states, "routes": routes, "router_weight": router_weight, "fc1_weight": fc1_weight, "fc2_weight": fc2_weight, "lengths": lengths, "lang_ids": lang_ids, "pivot_states": pivot_states, "query_weight": query_weight, "key_weight": key_weight, "value_weight": value_weight, "out_weight": out_weight}


EPSILON = 1e-05
NEGATIVE = -1e+30

def normalize(values):
    values = values.astype(jnp.float32)
    center = lax.optimization_barrier(jnp.mean(values, axis=-1, keepdims=True))
    shifted = values - center
    spread = lax.optimization_barrier(jnp.mean(shifted * shifted, axis=-1, keepdims=True))
    return shifted * lax.rsqrt(spread + EPSILON)

def run_expert(packed):
    row_block, weight_in, weight_back = packed
    hidden = jnp.maximum(jnp.dot(row_block, weight_in, preferred_element_type=jnp.float32), 0.0).astype(jnp.bfloat16)
    slice_width = FF // SLICES
    summed = jnp.zeros((row_block.shape[0], D), jnp.float32)
    for slice_index in range(SLICES):
        lower = slice_index * slice_width
        slice_term = jnp.dot(hidden[:, lower:lower + slice_width], weight_back[lower:lower + slice_width], preferred_element_type=jnp.float32)
        summed = summed + lax.optimization_barrier(slice_term.astype(jnp.bfloat16)).astype(jnp.float32)
    return summed.astype(jnp.bfloat16)

def decode_block(packed, pivot_states, query_weight, key_weight, value_weight, out_weight):
    encoded, block_lengths, block_langs = packed
    key_cache = jnp.dot(encoded, key_weight, preferred_element_type=jnp.float32).astype(jnp.bfloat16)
    value_cache = jnp.dot(encoded, value_weight, preferred_element_type=jnp.float32).astype(jnp.bfloat16)
    query_ends = jnp.cumsum(block_lengths).astype(jnp.int32)
    positions = jnp.arange(TOK_DEV, dtype=jnp.int32)
    key_owner = lax.optimization_barrier(jnp.sum((positions[:, None] >= query_ends[None, :]).astype(jnp.int32), axis=1))
    row_owner = jnp.arange(QRY * PIVOTS, dtype=jnp.int32) // PIVOTS
    allowed = row_owner[:, None] == key_owner[None, :]
    language_pick = (block_langs.reshape(-1)[:, None] == jnp.arange(PIVOTS, dtype=jnp.int32)[None, :]).astype(jnp.bfloat16)
    decoder_in = jnp.dot(language_pick, pivot_states, preferred_element_type=jnp.float32).astype(jnp.bfloat16)
    queries = jnp.dot(decoder_in, query_weight, preferred_element_type=jnp.float32).astype(jnp.bfloat16)
    query_heads = queries.reshape(QRY * PIVOTS, HEADS, HD).astype(jnp.float32)
    key_heads = key_cache.reshape(TOK_DEV, HEADS, HD).astype(jnp.float32)
    value_heads = value_cache.reshape(TOK_DEV, HEADS, HD).astype(jnp.float32)
    scores = jnp.einsum('rhe,the->hrt', query_heads, key_heads) * HD ** (-0.5)
    scores = jnp.where(allowed[None], scores, NEGATIVE)
    row_max = lax.optimization_barrier(jnp.max(scores, axis=2, keepdims=True))
    weights = jnp.exp(scores - row_max)
    attention = (weights / lax.optimization_barrier(jnp.sum(weights, axis=2, keepdims=True))).astype(jnp.bfloat16)
    context = jnp.einsum('hrt,the->rhe', attention.astype(jnp.float32), value_heads).astype(jnp.bfloat16)
    attended = jnp.dot(context.reshape(QRY * PIVOTS, D), out_weight, preferred_element_type=jnp.float32)
    return normalize(decoder_in.astype(jnp.float32) + attended).astype(jnp.bfloat16)

def reference(source_states, routes, router_weight, fc1_weight, fc2_weight, lengths, lang_ids, pivot_states, query_weight, key_weight, value_weight, out_weight):
    normed = normalize(source_states).astype(jnp.bfloat16)
    logits = jnp.dot(normed, router_weight, preferred_element_type=jnp.float32)
    expert_iota = jnp.arange(EXPERTS, dtype=jnp.int32)
    chosen = routes[:, :, None] == expert_iota[None, None, :]
    pair_logits = lax.optimization_barrier(jnp.sum(jnp.where(chosen, logits[:, None, :], 0.0), axis=2))
    gate_values = jax.nn.sigmoid(pair_logits - pair_logits[:, ::-1])
    blocked = chosen.reshape(QBLOCKS, TOK_DEV * 2, EXPERTS).astype(jnp.int32)
    before = jnp.cumsum(blocked, axis=1) - blocked
    slots = lax.optimization_barrier(jnp.sum(before * blocked, axis=2)).reshape(TOKENS, 2).astype(jnp.int32)
    block_index = jnp.arange(TOKENS, dtype=jnp.int32) // TOK_DEV
    block_pair = jnp.broadcast_to(block_index[:, None], (TOKENS, 2)).astype(jnp.int32)
    buffer = jnp.zeros((EXPERTS, QBLOCKS, CAP, D), jnp.bfloat16)
    buffer = buffer.at[routes, block_pair, slots].set(jnp.broadcast_to(normed[:, None, :], (TOKENS, 2, D)))
    results = lax.map(run_expert, (buffer.reshape(EXPERTS, QBLOCKS * CAP, D), fc1_weight, fc2_weight))
    results = results.reshape(EXPERTS, QBLOCKS, CAP, D)
    routed = results[routes, block_pair, slots].astype(jnp.float32)
    encoded_states = (source_states.astype(jnp.float32) + lax.optimization_barrier(jnp.sum(gate_values[:, :, None] * routed, axis=1))).astype(jnp.bfloat16)

    def one_block(packed):
        return decode_block(packed, pivot_states, query_weight, key_weight, value_weight, out_weight)
    decoded = lax.map(one_block, (encoded_states.reshape(QBLOCKS, TOK_DEV, D), lengths, lang_ids.reshape(QBLOCKS, QRY, PIVOTS)))
    return (encoded_states, decoded.reshape(ROWS, D))
```

```python
import functools

import jax
import jax.numpy as jnp
from jax import lax
from jax.experimental import pallas as pl
from jax.experimental.pallas import tpu as pltpu
from jax.sharding import PartitionSpec as P

HD = 128


EPSILON = 1e-05
NEGATIVE = -1e30


def normalize(values):
    values = values.astype(jnp.float32)
    center = jnp.mean(values, axis=-1, keepdims=True)
    shifted = values - center
    spread = jnp.mean(shifted * shifted, axis=-1, keepdims=True)
    return shifted * lax.rsqrt(spread + EPSILON)


def route_tables(routes, experts, capacity):
    tok_count = routes.shape[0]
    expert_iota = jnp.arange(experts, dtype=jnp.int32)
    chosen = routes[:, :, None] == expert_iota[None, None, :]
    flat_chosen = chosen.reshape(tok_count * 2, experts).astype(jnp.bfloat16)
    pair_iota = jnp.arange(tok_count * 2, dtype=jnp.int32)
    earlier = (pair_iota[None, :] < pair_iota[:, None]).astype(jnp.bfloat16)
    before = jnp.dot(earlier, flat_chosen, preferred_element_type=jnp.float32)
    slots = jnp.sum(before * flat_chosen.astype(jnp.float32), axis=1)
    slots = slots.astype(jnp.int32).reshape(tok_count, 2)
    slot_iota = jnp.arange(capacity, dtype=jnp.int32)
    placed = chosen[:, :, :, None] & (slots[:, :, None, None] == slot_iota[None, None, None, :])
    return (chosen, placed.reshape(tok_count, 2, experts * capacity).astype(jnp.bfloat16))


def project_pair(key_weight, value_weight):

    def project(totals, shard_part, offset):
        return (
            jnp.dot(shard_part, key_weight, preferred_element_type=jnp.float32),
            jnp.dot(shard_part, value_weight, preferred_element_type=jnp.float32),
        )

    return project


def packed_shards(
    source_states,
    routes,
    router_weight,
    fc1_weight,
    fc2_weight,
    lengths,
    lang_ids,
    pivot_states,
    query_weight,
    key_weight,
    value_weight,
    out_weight,
):
    tok_count, model_width = source_states.shape
    experts = router_weight.shape[1]
    capacity = 4 * tok_count // experts
    tensor_count = lax.axis_size("tensor")
    column_width = model_width // tensor_count
    column_start = lax.axis_index("tensor") * column_width
    normed = normalize(source_states).astype(jnp.bfloat16)
    logits = jnp.dot(normed, router_weight, preferred_element_type=jnp.float32)
    chosen, placed = route_tables(routes, experts, capacity)
    pair_logits = jnp.sum(jnp.where(chosen, logits[:, None, :], 0.0), axis=2)
    gate_values = jax.nn.sigmoid(pair_logits - pair_logits[:, ::-1])
    occupied = jnp.sum(placed, axis=1)
    outgoing = jnp.einsum("ts,td->sd", occupied, normed, preferred_element_type=jnp.float32)
    outgoing = outgoing.astype(jnp.bfloat16).reshape(experts, capacity, model_width)
    weight_in = fc1_weight[0]
    weight_back = fc2_weight[0]
    arrived = lax.all_to_all(outgoing, "expert", split_axis=0, concat_axis=0, tiled=True)
    row_block = arrived.reshape(-1, model_width)
    hidden = jnp.maximum(
        jnp.dot(row_block, weight_in, preferred_element_type=jnp.float32), 0.0
    ).astype(jnp.bfloat16)
    partial_value = jnp.dot(hidden, weight_back, preferred_element_type=jnp.float32).astype(
        jnp.bfloat16
    )
    partials = partial_value.reshape(arrived.shape)
    zeroed = jnp.zeros((tok_count, key_weight.shape[1]), jnp.float32)
    project = project_pair(key_weight, value_weight)
    own_cols = lax.dynamic_slice_in_dim(source_states, column_start, column_width, 1).astype(
        jnp.float32
    )
    widened = partials.astype(jnp.float32)
    summed = lax.psum_scatter(
        widened.astype(jnp.bfloat16), "tensor", scatter_dimension=2, tiled=True
    )
    returned_rows = lax.all_to_all(summed, "expert", split_axis=0, concat_axis=0, tiled=True)
    picked = jnp.einsum(
        "tks,sd->tkd",
        placed,
        returned_rows.reshape(experts * capacity, column_width),
        preferred_element_type=jnp.float32,
    )
    encoded = (own_cols + jnp.sum(gate_values[:, :, None] * picked, axis=1)).astype(jnp.bfloat16)
    key_sum, value_sum = project(
        (zeroed, zeroed), lax.all_gather(encoded, "tensor", axis=1, tiled=True), jnp.int32(0)
    )
    key_cache = key_sum.astype(jnp.bfloat16)
    value_cache = value_sum.astype(jnp.bfloat16)
    query_count = lengths.shape[1]
    pivot_count = pivot_states.shape[0]
    row_count = query_count * pivot_count
    query_iota = jnp.arange(query_count, dtype=jnp.int32)
    query_ends = jnp.sum(
        jnp.where(query_iota[None, :] <= query_iota[:, None], lengths[0][None, :], 0), axis=1
    )
    positions = jnp.arange(tok_count, dtype=jnp.int32)
    key_owner = jnp.sum((positions[:, None] >= query_ends[None, :]).astype(jnp.int32), axis=1)
    row_owner = jnp.arange(row_count, dtype=jnp.int32) // pivot_count
    allowed = row_owner[:, None] == key_owner[None, :]
    language_pick = (
        lang_ids.reshape(-1)[:, None] == jnp.arange(pivot_count, dtype=jnp.int32)[None, :]
    ).astype(jnp.bfloat16)
    decoder_in = jnp.dot(language_pick, pivot_states, preferred_element_type=jnp.float32).astype(
        jnp.bfloat16
    )
    queries = jnp.dot(decoder_in, query_weight, preferred_element_type=jnp.float32).astype(
        jnp.bfloat16
    )
    head_local = queries.shape[1] // HD
    query_heads = queries.reshape(row_count, head_local, HD)
    key_heads = key_cache.reshape(tok_count, head_local, HD)
    value_heads = value_cache.reshape(tok_count, head_local, HD)
    scores = jnp.einsum(
        "rhe,the->hrt", query_heads, key_heads, preferred_element_type=jnp.float32
    ) * HD ** (-0.5)
    scores = jnp.where(allowed[None], scores, NEGATIVE)
    row_max = jnp.max(scores, axis=2, keepdims=True)
    weights = jnp.exp(scores - row_max)
    attention = (weights / jnp.sum(weights, axis=2, keepdims=True)).astype(jnp.bfloat16)
    context = jnp.einsum(
        "hrt,the->rhe", attention, value_heads, preferred_element_type=jnp.float32
    ).astype(jnp.bfloat16)
    partial_out = jnp.dot(
        context.reshape(row_count, head_local * HD), out_weight, preferred_element_type=jnp.float32
    )
    attn_total = lax.psum(partial_out.astype(jnp.bfloat16), "tensor").astype(jnp.float32)
    decoded = normalize(decoder_in.astype(jnp.float32) + attn_total).astype(jnp.bfloat16)
    return (encoded, decoded)


MESH = pl.DeviceIdType.MESH
TILE = 256


def layer_kernel(
    experts,
    chips,
    normed,
    own_cols,
    gates,
    decoder_in,
    queries,
    mask,
    fc1_hbm,
    fc2_hbm,
    key_hbm,
    value_hbm,
    out_hbm,
    encoded,
    decoded,
    fc1,
    fc2,
    key_w,
    value_w,
    out_w,
    rows,
    hidden,
    core_out,
    core_in,
    kept,
    chip_out,
    chip_in,
    back_out,
    back_in,
    gathered,
    key_sum,
    value_sum,
    context,
    out_sum,
    half_out,
    half_in,
    sum_out,
    sum_in,
    full_in,
    load_sem,
    own_sem,
    up_sem,
    down_sem,
    line_recv,
    send_sem,
    recv_sem,
    ret_send,
    ret_recv,
    gat_send,
    gat_recv,
    end_send,
    end_recv,
):
    tokens, width = normed.shape
    columns = own_cols.shape[1]
    e = lax.axis_index("expert")
    t = lax.axis_index("tensor")
    chip, core = t // 2, t % 2
    mate = chip * 2 + 1 - core
    far = (1 - chip) * 2 + core
    far_mate = (1 - chip) * 2 + 1 - core
    tensor_peer = {"mate": {"tensor": mate}, "far": {"tensor": far}}

    def same(i):
        return 1 - ((e - i + experts) % experts + experts - 1) // experts

    nearest = [sorted(range(experts), key=lambda b, i=i: abs(b - i)) for i in range(experts)]
    order = [sum(same(i) * nearest[i][s] for i in range(experts)) for s in range(experts)]

    loads = [
        pltpu.make_async_copy(src, dst, load_sem.at[i])
        for i, (src, dst) in enumerate(
            ((fc1_hbm, fc1), (fc2_hbm, fc2), (key_hbm, key_w), (value_hbm, value_w), (out_hbm, out_w))
        )
    ]
    for load in loads:
        load.start()

    barrier = pltpu.get_barrier_semaphore()
    for step in range(1, experts):
        pl.semaphore_signal(
            barrier, 1, device_id={"expert": (e + step) % experts}, device_id_type=MESH
        )
    for peer in tensor_peer.values():
        pl.semaphore_signal(barrier, 1, device_id=peer, device_id_type=MESH)

    def quarter(q):
        return pl.ds(pl.multiple_of(q * columns, columns), columns)

    pl.semaphore_wait(barrier, experts + 1)

    def line(b, up, from_own):
        src = normed.at[:, quarter(t)] if from_own else rows.at[b, :, quarter(t)]
        return pltpu.make_async_remote_copy(
            src_ref=src,
            dst_ref=rows.at[b, :, quarter(t)],
            send_sem=(up_sem if up else down_sem).at[b],
            recv_sem=line_recv.at[b],
            device_id={"expert": (e + 1) % experts if up else (e + experts - 1) % experts},
            device_id_type=MESH,
        )

    def spread(b, q, kind, peer):
        return pltpu.make_async_remote_copy(
            src_ref=rows.at[b, :, quarter(q)],
            dst_ref=rows.at[b, :, quarter(q)],
            send_sem=send_sem.at[kind, b],
            recv_sem=recv_sem.at[kind, b],
            device_id=tensor_peer[peer],
            device_id_type=MESH,
        )

    @pl.when(e + 1 < experts)
    def _():
        line(e, True, True).start()

    @pl.when(e > 0)
    def _():
        line(e, False, True).start()

    def own_copy():
        return pltpu.make_async_copy(normed, rows.at[e], own_sem)

    own_copy().start()

    def arrive(s):
        b = order[s]
        line(b, True, False).wait_recv()

        @pl.when((b < e) & (e + 1 < experts))
        def _():
            line(b, True, False).start()

        @pl.when((b > e) & (e > 0))
        def _():
            line(b, False, False).start()

        spread(b, t, 0, "far").start()
        spread(b, t, 1, "mate").start()

    def relay(s):
        b = order[s]
        spread(b, far, 0, "far").wait_recv()
        spread(b, far, 2, "mate").start()

    def ready(s):
        b = order[s]
        spread(b, mate, 1, "mate").wait_recv()
        spread(b, far_mate, 2, "mate").wait_recv()

    def first(s):
        b = order[s]

        @pl.loop(0, hidden.shape[1] // TILE)
        def _(j):
            at = pl.ds(pl.multiple_of(j * TILE, TILE), TILE)
            tile = jnp.dot(rows[b], fc1[:, at], preferred_element_type=jnp.float32)
            hidden[:, at] = jnp.maximum(tile, 0.0).astype(jnp.bfloat16)

    per = columns // TILE

    def second(s):
        @pl.loop(0, chips * per)
        def _(j):
            p, k = j // per, j % per
            start = (p * 2 + 1 - core) * columns + k * TILE
            at = pl.ds(pl.multiple_of(start, TILE), TILE)
            tile = jnp.dot(hidden[...], fc2[:, at], preferred_element_type=jnp.float32)
            core_out[s, p, :, pl.ds(pl.multiple_of(k * TILE, TILE), TILE)] = tile.astype(
                jnp.bfloat16
            )

        pair_copy(s).start()

        @pl.loop(0, chips * per)
        def _(j):
            p, k = j // per, j % per
            start = (p * 2 + core) * columns + k * TILE
            at = pl.ds(pl.multiple_of(start, TILE), TILE)
            tile = jnp.dot(hidden[...], fc2[:, at], preferred_element_type=jnp.float32)
            kept[s, p, :, pl.ds(pl.multiple_of(k * TILE, TILE), TILE)] = tile

    def pair_copy(s):
        return pltpu.make_async_remote_copy(
            src_ref=core_out.at[s],
            dst_ref=core_in.at[s],
            send_sem=ret_send.at[0, s],
            recv_sem=ret_recv.at[0, s],
            device_id=tensor_peer["mate"],
            device_id_type=MESH,
        )

    def chip_copy(s):
        return pltpu.make_async_remote_copy(
            src_ref=chip_out.at[s],
            dst_ref=chip_in.at[s],
            send_sem=ret_send.at[1, s],
            recv_sem=ret_recv.at[1, s],
            device_id=tensor_peer["far"],
            device_id_type=MESH,
        )

    def back_copy(s, b):
        return pltpu.make_async_remote_copy(
            src_ref=back_out.at[s],
            dst_ref=back_in.at[e],
            send_sem=ret_send.at[2, s],
            recv_sem=ret_recv.at[2, e],
            device_id={"expert": b},
            device_id_type=MESH,
        )

    def back_wait(i):
        return pltpu.make_async_remote_copy(
            src_ref=back_out.at[0],
            dst_ref=back_in.at[i],
            send_sem=ret_send.at[2, 0],
            recv_sem=ret_recv.at[2, i],
            device_id={"expert": i},
            device_id_type=MESH,
        )

    def reduce_pair(s):
        pair_copy(s).wait_recv()
        other = 1 - chip
        chip_out[s] = (kept[s, other] + core_in[s, other].astype(jnp.float32)).astype(jnp.bfloat16)
        chip_copy(s).start()

    def reduce_chips(s):
        chip_copy(s).wait_recv()
        total = (
            kept[s, chip]
            + core_in[s, chip].astype(jnp.float32)
            + chip_in[s].astype(jnp.float32)
        ).astype(jnp.bfloat16)
        if s == 0:
            back_in[e] = total
        else:
            back_out[s] = total
            back_copy(s, order[s]).start()

    own_copy().wait()
    loads[0].wait()
    first(0)
    arrive(1)
    loads[1].wait()
    second(0)
    arrive(2)
    relay(1)
    reduce_pair(0)
    ready(1)
    first(1)
    arrive(3)
    relay(2)
    second(1)
    reduce_chips(0)
    reduce_pair(1)
    relay(3)
    ready(2)
    first(2)
    second(2)
    reduce_chips(1)
    reduce_pair(2)
    ready(3)
    first(3)
    reduce_chips(2)
    second(3)
    reduce_pair(3)
    reduce_chips(3)

    for s in range(1, experts):
        back_wait(order[s]).wait_recv()
    mixed = own_cols[...].astype(jnp.float32)
    for i in range(experts):
        mixed = mixed + gates[:, i : i + 1] * back_in[i].astype(jnp.float32)
    mixed = mixed.astype(jnp.bfloat16)
    encoded[...] = mixed
    gathered[:, quarter(t)] = mixed

    def gather(q, kind, peer):
        return pltpu.make_async_remote_copy(
            src_ref=gathered.at[:, quarter(q)],
            dst_ref=gathered.at[:, quarter(q)],
            send_sem=gat_send.at[kind],
            recv_sem=gat_recv.at[kind],
            device_id=tensor_peer[peer],
            device_id_type=MESH,
        )

    gather(t, 0, "far").start()
    gather(t, 1, "mate").start()
    for load in loads[2:]:
        load.wait()

    def project(q, fresh):
        part = gathered[:, quarter(q)]
        for weight, total in ((key_w, key_sum), (value_w, value_sum)):
            term = jnp.dot(part, weight[quarter(q), :], preferred_element_type=jnp.float32)
            total[...] = term if fresh else total[...] + term

    project(t, True)
    gather(mate, 1, "mate").wait_recv()
    project(mate, False)
    gather(far, 0, "far").wait_recv()
    gather(far, 2, "mate").start()
    project(far, False)
    gather(far_mate, 2, "mate").wait_recv()
    project(far_mate, False)

    for h in range(columns // HD):
        at = slice(h * HD, (h + 1) * HD)
        scores = lax.dot_general(
            queries[:, at],
            key_sum[:, at].astype(jnp.bfloat16),
            (((1,), (1,)), ((), ())),
            preferred_element_type=jnp.float32,
        ) * HD ** (-0.5)
        scores = jnp.where(mask[...] > 0.5, scores, NEGATIVE)
        weights = jnp.exp(scores - jnp.max(scores, axis=1, keepdims=True))
        attention = (weights / jnp.sum(weights, axis=1, keepdims=True)).astype(jnp.bfloat16)
        context[:, at] = jnp.dot(
            attention, value_sum[:, at].astype(jnp.bfloat16), preferred_element_type=jnp.float32
        ).astype(jnp.bfloat16)

    half = width // 2

    def side(c):
        return pl.ds(pl.multiple_of(c * half, half), half)

    out_sum[...] = jnp.dot(context[...], out_w[...], preferred_element_type=jnp.float32)
    half_out[...] = out_sum[:, side(1 - core)].astype(jnp.bfloat16)

    def end_copy(src, dst, kind, peer):
        return pltpu.make_async_remote_copy(
            src_ref=src,
            dst_ref=dst,
            send_sem=end_send.at[kind],
            recv_sem=end_recv.at[kind],
            device_id=tensor_peer[peer],
            device_id_type=MESH,
        )

    ends = (
        end_copy(half_out, half_in, 0, "mate"),
        end_copy(sum_out, sum_in, 1, "far"),
        end_copy(full_in.at[core], full_in.at[core], 2, "mate"),
    )
    ends[0].start()
    ends[0].wait_recv()
    pair_sum = out_sum[:, side(core)] + half_in[...].astype(jnp.float32)
    sum_out[...] = pair_sum.astype(jnp.bfloat16)
    ends[1].start()
    ends[1].wait_recv()
    full_in[core] = (pair_sum + sum_in[...].astype(jnp.float32)).astype(jnp.bfloat16)
    ends[2].start()
    end_copy(full_in.at[core], full_in.at[1 - core], 2, "mate").wait_recv()
    total = jnp.concatenate([full_in[0], full_in[1]], axis=1).astype(jnp.float32)
    decoded[...] = normalize(decoder_in[...].astype(jnp.float32) + total).astype(jnp.bfloat16)

    @pl.when(e + 1 < experts)
    def _():
        line(e, True, True).wait_send()

    @pl.when(e > 0)
    def _():
        line(e, False, True).wait_send()

    for s in range(experts):
        b = order[s]
        if s > 0:

            @pl.when((b < e) & (e + 1 < experts))
            def _():
                line(b, True, False).wait_send()

            @pl.when((b > e) & (e > 0))
            def _():
                line(b, False, False).wait_send()

            spread(b, t, 0, "far").wait_send()
            spread(b, t, 1, "mate").wait_send()
            spread(b, far, 2, "mate").wait_send()
            back_copy(s, b).wait_send()
        pair_copy(s).wait_send()
        chip_copy(s).wait_send()
    gather(t, 0, "far").wait_send()
    gather(t, 1, "mate").wait_send()
    gather(far, 2, "mate").wait_send()
    for end in ends:
        end.wait_send()


def dense_shards(
    source_states,
    routes,
    router_weight,
    fc1_weight,
    fc2_weight,
    lengths,
    lang_ids,
    pivot_states,
    query_weight,
    key_weight,
    value_weight,
    out_weight,
):
    tok_count, model_width = source_states.shape
    experts = router_weight.shape[1]
    tensor_count = lax.axis_size("tensor")
    chips = tensor_count // 2
    columns = model_width // tensor_count
    normed = normalize(source_states).astype(jnp.bfloat16)
    logits = jnp.dot(normed, router_weight, preferred_element_type=jnp.float32)
    chosen = routes[:, :, None] == jnp.arange(experts, dtype=jnp.int32)[None, None, :]
    pair_logits = jnp.sum(jnp.where(chosen, logits[:, None, :], 0.0), axis=2)
    gate_values = jax.nn.sigmoid(pair_logits - pair_logits[:, ::-1])
    gates = jnp.sum(jnp.where(chosen, gate_values[:, :, None], 0.0), axis=1)
    own_cols = lax.dynamic_slice_in_dim(
        source_states, lax.axis_index("tensor") * columns, columns, 1
    )
    query_count = lengths.shape[1]
    pivot_count = pivot_states.shape[0]
    row_count = query_count * pivot_count
    query_iota = jnp.arange(query_count, dtype=jnp.int32)
    query_ends = jnp.sum(
        jnp.where(query_iota[None, :] <= query_iota[:, None], lengths[0][None, :], 0), axis=1
    )
    positions = jnp.arange(tok_count, dtype=jnp.int32)
    key_owner = jnp.sum((positions[:, None] >= query_ends[None, :]).astype(jnp.int32), axis=1)
    row_owner = jnp.arange(row_count, dtype=jnp.int32) // pivot_count
    mask = (row_owner[:, None] == key_owner[None, :]).astype(jnp.float32)
    language_pick = (
        lang_ids.reshape(-1)[:, None] == jnp.arange(pivot_count, dtype=jnp.int32)[None, :]
    ).astype(jnp.bfloat16)
    decoder_in = jnp.dot(language_pick, pivot_states, preferred_element_type=jnp.float32).astype(
        jnp.bfloat16
    )
    queries = jnp.dot(decoder_in, query_weight, preferred_element_type=jnp.float32).astype(
        jnp.bfloat16
    )
    vmem = pl.BlockSpec(memory_space=pltpu.VMEM)
    hbm = pl.BlockSpec(memory_space=pl.ANY)
    bf16, f32, dma = jnp.bfloat16, jnp.float32, pltpu.SemaphoreType.DMA
    units = fc1_weight.shape[2]
    half = model_width // 2
    return pl.pallas_call(
        functools.partial(layer_kernel, experts, chips),
        out_shape=(
            jax.ShapeDtypeStruct((tok_count, columns), bf16),
            jax.ShapeDtypeStruct((row_count, model_width), bf16),
        ),
        in_specs=[vmem] * 6 + [hbm] * 5,
        out_specs=(vmem, vmem),
        scratch_shapes=[
            pltpu.VMEM((model_width, units), bf16),
            pltpu.VMEM((units, model_width), bf16),
            pltpu.VMEM((model_width, columns), bf16),
            pltpu.VMEM((model_width, columns), bf16),
            pltpu.VMEM((columns, model_width), bf16),
            pltpu.VMEM((experts, tok_count, model_width), bf16),
            pltpu.VMEM((tok_count, units), bf16),
            pltpu.VMEM((experts, chips, tok_count, columns), bf16),
            pltpu.VMEM((experts, chips, tok_count, columns), bf16),
            pltpu.VMEM((experts, chips, tok_count, columns), f32),
            pltpu.VMEM((experts, tok_count, columns), bf16),
            pltpu.VMEM((experts, tok_count, columns), bf16),
            pltpu.VMEM((experts, tok_count, columns), bf16),
            pltpu.VMEM((experts, tok_count, columns), bf16),
            pltpu.VMEM((tok_count, model_width), bf16),
            pltpu.VMEM((tok_count, columns), f32),
            pltpu.VMEM((tok_count, columns), f32),
            pltpu.VMEM((row_count, columns), bf16),
            pltpu.VMEM((row_count, model_width), f32),
            pltpu.VMEM((row_count, half), bf16),
            pltpu.VMEM((row_count, half), bf16),
            pltpu.VMEM((row_count, half), bf16),
            pltpu.VMEM((row_count, half), bf16),
            pltpu.VMEM((2, row_count, half), bf16),
            dma((5,)),
            dma,
            dma((experts,)),
            dma((experts,)),
            dma((experts,)),
            dma((3, experts)),
            dma((3, experts)),
            dma((3, experts)),
            dma((3, experts)),
            dma((3,)),
            dma((3,)),
            dma((3,)),
            dma((3,)),
        ],
        compiler_params=pltpu.CompilerParams(
            collective_id=0, has_side_effects=True, vmem_limit_bytes=60 * 2**20
        ),
    )(
        normed,
        own_cols,
        gates,
        decoder_in,
        queries,
        mask,
        fc1_weight[0],
        fc2_weight[0],
        key_weight,
        value_weight,
        out_weight,
    )


def solution(mesh):
    in_specs = (
        P(("groups", "expert"), None),
        P(("groups", "expert"), None),
        P(),
        P("expert", None, "tensor"),
        P("expert", "tensor", None),
        P(("groups", "expert"), None),
        P(("groups", "expert"), None),
        P(),
        P(None, "tensor"),
        P(None, "tensor"),
        P(None, "tensor"),
        P("tensor", None),
    )
    out_specs = (P(("groups", "expert"), "tensor"), P(("groups", "expert"), None))
    sizes = dict(mesh.shape)
    shards = dense_shards if sizes["expert"] == 4 and sizes["tensor"] == 4 else packed_shards
    return jax.shard_map(shards, mesh=mesh, in_specs=in_specs, out_specs=out_specs, check_vma=False)
```

```python
import functools

import jax
import jax.numpy as jnp
from jax import lax
from jax.experimental import pallas as pl
from jax.experimental.pallas import tpu as pltpu
from jax.sharding import PartitionSpec as P

HD = 128


EPSILON = 1e-05
NEGATIVE = -1e30


def normalize(values):
    values = values.astype(jnp.float32)
    center = jnp.mean(values, axis=-1, keepdims=True)
    shifted = values - center
    spread = jnp.mean(shifted * shifted, axis=-1, keepdims=True)
    return shifted * lax.rsqrt(spread + EPSILON)


def route_tables(routes, experts, capacity):
    tok_count = routes.shape[0]
    expert_iota = jnp.arange(experts, dtype=jnp.int32)
    chosen = routes[:, :, None] == expert_iota[None, None, :]
    flat_chosen = chosen.reshape(tok_count * 2, experts).astype(jnp.bfloat16)
    pair_iota = jnp.arange(tok_count * 2, dtype=jnp.int32)
    earlier = (pair_iota[None, :] < pair_iota[:, None]).astype(jnp.bfloat16)
    before = jnp.dot(earlier, flat_chosen, preferred_element_type=jnp.float32)
    slots = jnp.sum(before * flat_chosen.astype(jnp.float32), axis=1)
    slots = slots.astype(jnp.int32).reshape(tok_count, 2)
    slot_iota = jnp.arange(capacity, dtype=jnp.int32)
    placed = chosen[:, :, :, None] & (slots[:, :, None, None] == slot_iota[None, None, None, :])
    return (chosen, placed.reshape(tok_count, 2, experts * capacity).astype(jnp.bfloat16))


def project_pair(key_weight, value_weight):

    def project(totals, shard_part, offset):
        return (
            jnp.dot(shard_part, key_weight, preferred_element_type=jnp.float32),
            jnp.dot(shard_part, value_weight, preferred_element_type=jnp.float32),
        )

    return project


def packed_shards(
    source_states,
    routes,
    router_weight,
    fc1_weight,
    fc2_weight,
    lengths,
    lang_ids,
    pivot_states,
    query_weight,
    key_weight,
    value_weight,
    out_weight,
):
    tok_count, model_width = source_states.shape
    experts = router_weight.shape[1]
    capacity = 4 * tok_count // experts
    tensor_count = lax.axis_size("tensor")
    column_width = model_width // tensor_count
    column_start = lax.axis_index("tensor") * column_width
    normed = normalize(source_states).astype(jnp.bfloat16)
    logits = jnp.dot(normed, router_weight, preferred_element_type=jnp.float32)
    chosen, placed = route_tables(routes, experts, capacity)
    pair_logits = jnp.sum(jnp.where(chosen, logits[:, None, :], 0.0), axis=2)
    gate_values = jax.nn.sigmoid(pair_logits - pair_logits[:, ::-1])
    occupied = jnp.sum(placed, axis=1)
    outgoing = jnp.einsum("ts,td->sd", occupied, normed, preferred_element_type=jnp.float32)
    outgoing = outgoing.astype(jnp.bfloat16).reshape(experts, capacity, model_width)
    weight_in = fc1_weight[0]
    weight_back = fc2_weight[0]
    arrived = lax.all_to_all(outgoing, "expert", split_axis=0, concat_axis=0, tiled=True)
    row_block = arrived.reshape(-1, model_width)
    hidden = jnp.maximum(
        jnp.dot(row_block, weight_in, preferred_element_type=jnp.float32), 0.0
    ).astype(jnp.bfloat16)
    partial_value = jnp.dot(hidden, weight_back, preferred_element_type=jnp.float32).astype(
        jnp.bfloat16
    )
    partials = partial_value.reshape(arrived.shape)
    zeroed = jnp.zeros((tok_count, key_weight.shape[1]), jnp.float32)
    project = project_pair(key_weight, value_weight)
    own_cols = lax.dynamic_slice_in_dim(source_states, column_start, column_width, 1).astype(
        jnp.float32
    )
    widened = partials.astype(jnp.float32)
    summed = lax.psum_scatter(
        widened.astype(jnp.bfloat16), "tensor", scatter_dimension=2, tiled=True
    )
    returned_rows = lax.all_to_all(summed, "expert", split_axis=0, concat_axis=0, tiled=True)
    picked = jnp.einsum(
        "tks,sd->tkd",
        placed,
        returned_rows.reshape(experts * capacity, column_width),
        preferred_element_type=jnp.float32,
    )
    encoded = (own_cols + jnp.sum(gate_values[:, :, None] * picked, axis=1)).astype(jnp.bfloat16)
    key_sum, value_sum = project(
        (zeroed, zeroed), lax.all_gather(encoded, "tensor", axis=1, tiled=True), jnp.int32(0)
    )
    key_cache = key_sum.astype(jnp.bfloat16)
    value_cache = value_sum.astype(jnp.bfloat16)
    query_count = lengths.shape[1]
    pivot_count = pivot_states.shape[0]
    row_count = query_count * pivot_count
    query_iota = jnp.arange(query_count, dtype=jnp.int32)
    query_ends = jnp.sum(
        jnp.where(query_iota[None, :] <= query_iota[:, None], lengths[0][None, :], 0), axis=1
    )
    positions = jnp.arange(tok_count, dtype=jnp.int32)
    key_owner = jnp.sum((positions[:, None] >= query_ends[None, :]).astype(jnp.int32), axis=1)
    row_owner = jnp.arange(row_count, dtype=jnp.int32) // pivot_count
    allowed = row_owner[:, None] == key_owner[None, :]
    language_pick = (
        lang_ids.reshape(-1)[:, None] == jnp.arange(pivot_count, dtype=jnp.int32)[None, :]
    ).astype(jnp.bfloat16)
    decoder_in = jnp.dot(language_pick, pivot_states, preferred_element_type=jnp.float32).astype(
        jnp.bfloat16
    )
    queries = jnp.dot(decoder_in, query_weight, preferred_element_type=jnp.float32).astype(
        jnp.bfloat16
    )
    head_local = queries.shape[1] // HD
    query_heads = queries.reshape(row_count, head_local, HD)
    key_heads = key_cache.reshape(tok_count, head_local, HD)
    value_heads = value_cache.reshape(tok_count, head_local, HD)
    scores = jnp.einsum(
        "rhe,the->hrt", query_heads, key_heads, preferred_element_type=jnp.float32
    ) * HD ** (-0.5)
    scores = jnp.where(allowed[None], scores, NEGATIVE)
    row_max = jnp.max(scores, axis=2, keepdims=True)
    weights = jnp.exp(scores - row_max)
    attention = (weights / jnp.sum(weights, axis=2, keepdims=True)).astype(jnp.bfloat16)
    context = jnp.einsum(
        "hrt,the->rhe", attention, value_heads, preferred_element_type=jnp.float32
    ).astype(jnp.bfloat16)
    partial_out = jnp.dot(
        context.reshape(row_count, head_local * HD), out_weight, preferred_element_type=jnp.float32
    )
    attn_total = lax.psum(partial_out.astype(jnp.bfloat16), "tensor").astype(jnp.float32)
    decoded = normalize(decoder_in.astype(jnp.float32) + attn_total).astype(jnp.bfloat16)
    return (encoded, decoded)


MESH = pl.DeviceIdType.MESH
TILE = 256


def layer_kernel(
    experts,
    chips,
    source,
    routes,
    router_w,
    lengths,
    languages,
    pivots,
    fc1_hbm,
    fc2_hbm,
    query_hbm,
    key_hbm,
    value_hbm,
    out_hbm,
    encoded,
    decoded,
    fc1,
    fc2,
    query_w,
    key_w,
    value_w,
    out_w,
    gates,
    decoder_in,
    queries,
    rows,
    hidden,
    core_out,
    core_in,
    kept,
    chip_out,
    chip_in,
    back_out,
    back_in,
    gathered,
    key_sum,
    value_sum,
    context,
    out_sum,
    half_out,
    half_in,
    sum_out,
    sum_in,
    full_in,
    load_sem,
    up_sem,
    down_sem,
    line_recv,
    send_sem,
    recv_sem,
    ret_send,
    ret_recv,
    gat_send,
    gat_recv,
    end_send,
    end_recv,
):
    tokens, width = source.shape
    columns = encoded.shape[1]
    parts = 2
    part_rows = tokens // parts
    per = columns // TILE
    e = lax.axis_index("expert")
    t = lax.axis_index("tensor")
    chip, core = t // 2, t % 2
    mate = chip * 2 + 1 - core
    far = (1 - chip) * 2 + core
    far_mate = (1 - chip) * 2 + 1 - core
    tensor_peer = {"mate": {"tensor": mate}, "far": {"tensor": far}}

    def same(i):
        return 1 - ((e - i + experts) % experts + experts - 1) // experts

    nearest = [sorted(range(experts), key=lambda b, i=i: abs(b - i)) for i in range(experts)]
    order = [sum(same(i) * nearest[i][s] for i in range(experts)) for s in range(experts)]

    loads = [
        pltpu.make_async_copy(src, dst, load_sem.at[i])
        for i, (src, dst) in enumerate(
            (
                (fc1_hbm, fc1),
                (fc2_hbm, fc2),
                (query_hbm, query_w),
                (key_hbm, key_w),
                (value_hbm, value_w),
                (out_hbm, out_w),
            )
        )
    ]
    for load in loads:
        load.start()

    barrier = pltpu.get_barrier_semaphore()
    for step in range(1, experts):
        pl.semaphore_signal(
            barrier, 1, device_id={"expert": (e + step) % experts}, device_id_type=MESH
        )
    for peer in tensor_peer.values():
        pl.semaphore_signal(barrier, 1, device_id=peer, device_id_type=MESH)

    def quarter(q):
        return pl.ds(pl.multiple_of(q * columns, columns), columns)

    rows[e] = normalize(source[...]).astype(jnp.bfloat16)
    pl.semaphore_wait(barrier, experts + 1)

    def line(b, up, h):
        piece = rows.at[b, pl.ds(h * part_rows, part_rows), quarter(t)]
        return pltpu.make_async_remote_copy(
            src_ref=piece,
            dst_ref=piece,
            send_sem=(up_sem if up else down_sem).at[b, h],
            recv_sem=line_recv.at[b, h],
            device_id={"expert": (e + 1) % experts if up else (e + experts - 1) % experts},
            device_id_type=MESH,
        )

    def spread(b, q, h, kind, peer):
        piece = rows.at[b, pl.ds(h * part_rows, part_rows), quarter(q)]
        return pltpu.make_async_remote_copy(
            src_ref=piece,
            dst_ref=piece,
            send_sem=send_sem.at[kind, b, h],
            recv_sem=recv_sem.at[kind, b, h],
            device_id=tensor_peer[peer],
            device_id_type=MESH,
        )

    @pl.when(e + 1 < experts)
    def _():
        for h in range(parts):
            line(e, True, h).start()

    @pl.when(e > 0)
    def _():
        for h in range(parts):
            line(e, False, h).start()

    def arrive(s, h):
        b = order[s]
        line(b, True, h).wait_recv()

        @pl.when((b < e) & (e + 1 < experts))
        def _():
            line(b, True, h).start()

        @pl.when((b > e) & (e > 0))
        def _():
            line(b, False, h).start()

        spread(b, t, h, 0, "far").start()
        spread(b, t, h, 1, "mate").start()

    def relay(s, h):
        b = order[s]
        spread(b, far, h, 0, "far").wait_recv()
        spread(b, far, h, 2, "mate").start()

    def ready(s):
        b = order[s]
        for h in range(parts):
            spread(b, mate, h, 1, "mate").wait_recv()
            spread(b, far_mate, h, 2, "mate").wait_recv()

    tiles = hidden.shape[1] // TILE

    def first(s, a):
        b = order[s]

        @pl.loop(a * (tiles // 2), (a + 1) * (tiles // 2))
        def _(j):
            at = pl.ds(pl.multiple_of(j * TILE, TILE), TILE)
            tile = jnp.dot(rows[b], fc1[:, at], preferred_element_type=jnp.float32)
            hidden[:, at] = jnp.maximum(tile, 0.0).astype(jnp.bfloat16)

    def second_tile(p, c, k):
        at = pl.ds(pl.multiple_of((p * 2 + c) * columns + k * TILE, TILE), TILE)
        return jnp.dot(hidden[...], fc2[:, at], preferred_element_type=jnp.float32)

    def second(s, k):
        @pl.loop(0, chips)
        def _(p):
            core_out[s, k, p] = second_tile(p, 1 - core, k).astype(jnp.bfloat16)

        pair_copy(s, k).start()

        @pl.loop(0, chips)
        def _(p):
            kept[s, k, p] = second_tile(p, core, k)

    def pair_copy(s, k):
        return pltpu.make_async_remote_copy(
            src_ref=core_out.at[s, k],
            dst_ref=core_in.at[s, k],
            send_sem=ret_send.at[0, s, k],
            recv_sem=ret_recv.at[0, s, k],
            device_id=tensor_peer["mate"],
            device_id_type=MESH,
        )

    def chip_copy(s, k):
        return pltpu.make_async_remote_copy(
            src_ref=chip_out.at[s, k],
            dst_ref=chip_in.at[s, k],
            send_sem=ret_send.at[1, s, k],
            recv_sem=ret_recv.at[1, s, k],
            device_id=tensor_peer["far"],
            device_id_type=MESH,
        )

    def back_copy(s, k):
        return pltpu.make_async_remote_copy(
            src_ref=back_out.at[s, k],
            dst_ref=back_in.at[e, k],
            send_sem=ret_send.at[2, s, k],
            recv_sem=ret_recv.at[2, e, k],
            device_id={"expert": order[s]},
            device_id_type=MESH,
        )

    def back_wait(i, k):
        return pltpu.make_async_remote_copy(
            src_ref=back_out.at[0, k],
            dst_ref=back_in.at[i, k],
            send_sem=ret_send.at[2, 0, k],
            recv_sem=ret_recv.at[2, i, k],
            device_id={"expert": i},
            device_id_type=MESH,
        )

    def reduce_pair(s, k):
        pair_copy(s, k).wait_recv()
        other = 1 - chip
        chip_out[s, k] = (
            kept[s, k, other] + core_in[s, k, other].astype(jnp.float32)
        ).astype(jnp.bfloat16)
        chip_copy(s, k).start()

    def reduce_chips(s, k):
        chip_copy(s, k).wait_recv()
        total = (
            kept[s, k, chip]
            + core_in[s, k, chip].astype(jnp.float32)
            + chip_in[s, k].astype(jnp.float32)
        ).astype(jnp.bfloat16)
        if s == 0:
            back_in[e, k] = total
        else:
            back_out[s, k] = total
            back_copy(s, k).start()

    def route():
        logits = jnp.dot(rows[e], router_w[...], preferred_element_type=jnp.float32)
        lane = lax.broadcasted_iota(jnp.int32, logits.shape, 1)
        chosen = [routes[:, i : i + 1] == lane for i in range(2)]
        picked = [jnp.sum(jnp.where(c, logits, 0.0), axis=1, keepdims=True) for c in chosen]
        difference = picked[0] - picked[1]
        gates[...] = jnp.where(chosen[0], jax.nn.sigmoid(difference), 0.0) + jnp.where(
            chosen[1], jax.nn.sigmoid(-difference), 0.0
        )

    query_count, pivot_count = languages.shape
    row_count = decoded.shape[0]

    def ask():
        place = lax.broadcasted_iota(jnp.int32, (row_count, query_count), 0)
        query = lax.broadcasted_iota(jnp.int32, (row_count, query_count), 1)
        below, above = query * pivot_count, (query + 1) * pivot_count
        owner = ((place >= below) & (place < above)).astype(jnp.float32)
        named = jnp.dot(
            owner, languages[...].astype(jnp.float32), preferred_element_type=jnp.float32
        )
        first_row = jnp.zeros((row_count, pivot_count), jnp.int32)
        place = lax.broadcasted_iota(jnp.int32, (row_count, pivot_count), 0)
        for i in range(1, query_count):
            first_row = first_row + jnp.where(place >= i * pivot_count, pivot_count, 0)
        lane = lax.broadcasted_iota(jnp.int32, (row_count, pivot_count), 1)
        language = jnp.sum(
            jnp.where(place - first_row == lane, named, 0.0), axis=1, keepdims=True
        )
        pick = (jnp.abs(language - lane.astype(jnp.float32)) < 0.5).astype(jnp.bfloat16)
        decoder_in[...] = jnp.dot(
            pick, pivots[...], preferred_element_type=jnp.float32
        ).astype(jnp.bfloat16)
        loads[2].wait()
        queries[...] = jnp.dot(
            decoder_in[...], query_w[...], preferred_element_type=jnp.float32
        ).astype(jnp.bfloat16)

    loads[0].wait()
    first(0, 0)
    first(0, 1)
    arrive(1, 0)
    loads[1].wait()
    second(0, 0)
    arrive(1, 1)
    second(0, 1)
    relay(1, 0)
    relay(1, 1)
    arrive(2, 0)
    route()
    arrive(2, 1)
    reduce_pair(0, 0)
    ready(1)
    first(1, 0)
    arrive(3, 0)
    relay(2, 0)
    first(1, 1)
    arrive(3, 1)
    relay(2, 1)
    reduce_pair(0, 1)
    second(1, 0)
    relay(3, 0)
    second(1, 1)
    reduce_pair(1, 0)
    relay(3, 1)
    reduce_chips(0, 0)
    reduce_pair(1, 1)
    ready(2)
    first(2, 0)
    reduce_chips(0, 1)
    first(2, 1)
    reduce_chips(1, 0)
    second(2, 0)
    reduce_chips(1, 1)
    second(2, 1)
    reduce_pair(2, 0)
    ready(3)
    first(3, 0)
    reduce_pair(2, 1)
    first(3, 1)
    reduce_chips(2, 0)
    second(3, 0)
    reduce_chips(2, 1)
    second(3, 1)
    reduce_pair(3, 0)
    reduce_pair(3, 1)
    reduce_chips(3, 0)
    reduce_chips(3, 1)
    ask()

    def part(q, k):
        return pl.ds(pl.multiple_of(q * columns + k * TILE, TILE), TILE)

    def gather(q, k, kind, peer):
        piece = gathered.at[:, part(q, k)]
        return pltpu.make_async_remote_copy(
            src_ref=piece,
            dst_ref=piece,
            send_sem=gat_send.at[kind, k],
            recv_sem=gat_recv.at[kind, k],
            device_id=tensor_peer[peer],
            device_id_type=MESH,
        )

    def project(q, k, fresh):
        piece = gathered[:, part(q, k)]
        for weight, total in ((key_w, key_sum), (value_w, value_sum)):
            term = jnp.dot(piece, weight[part(q, k), :], preferred_element_type=jnp.float32)
            total[...] = term if fresh else total[...] + term

    for load in loads[3:]:
        load.wait()
    for k in range(per):
        for s in range(1, experts):
            back_wait(order[s], k).wait_recv()
        mixed = source[:, part(t, k)].astype(jnp.float32)
        for i in range(experts):
            mixed = mixed + gates[:, i : i + 1] * back_in[i, k].astype(jnp.float32)
        mixed = mixed.astype(jnp.bfloat16)
        gathered[:, part(t, k)] = mixed
        gather(t, k, 0, "far").start()
        gather(t, k, 1, "mate").start()
        encoded[:, k * TILE : (k + 1) * TILE] = mixed
        project(t, k, k == 0)
    for k in range(per):
        gather(mate, k, 1, "mate").wait_recv()
        gather(far, k, 0, "far").wait_recv()
        gather(far, k, 2, "mate").start()
        project(mate, k, False)
        project(far, k, False)
    for k in range(per):
        gather(far_mate, k, 2, "mate").wait_recv()
        project(far_mate, k, False)

    position = lax.broadcasted_iota(jnp.int32, (row_count, tokens), 1)
    place = lax.broadcasted_iota(jnp.int32, (row_count, tokens), 0)
    end = jnp.zeros((1, 1), jnp.int32)
    allowed = jnp.zeros((row_count, tokens), jnp.float32)
    for i in range(query_count):
        begin, end = end, end + lengths[:, i : i + 1]
        inside = (position >= begin) & (position < end)
        inside = inside & (place >= i * pivot_count) & (place < (i + 1) * pivot_count)
        allowed = jnp.where(inside, 1.0, allowed)

    for h in range(columns // HD):
        at = slice(h * HD, (h + 1) * HD)
        scores = lax.dot_general(
            queries[:, at],
            key_sum[:, at].astype(jnp.bfloat16),
            (((1,), (1,)), ((), ())),
            preferred_element_type=jnp.float32,
        ) * HD ** (-0.5)
        scores = jnp.where(allowed > 0.5, scores, NEGATIVE)
        weights = jnp.exp(scores - jnp.max(scores, axis=1, keepdims=True))
        attention = (weights / jnp.sum(weights, axis=1, keepdims=True)).astype(jnp.bfloat16)
        context[:, at] = jnp.dot(
            attention, value_sum[:, at].astype(jnp.bfloat16), preferred_element_type=jnp.float32
        ).astype(jnp.bfloat16)

    half = width // 2

    def side(c):
        return pl.ds(pl.multiple_of(c * half, half), half)

    out_sum[...] = jnp.dot(context[...], out_w[...], preferred_element_type=jnp.float32)
    half_out[...] = out_sum[:, side(1 - core)].astype(jnp.bfloat16)

    def end_copy(src, dst, kind, peer):
        return pltpu.make_async_remote_copy(
            src_ref=src,
            dst_ref=dst,
            send_sem=end_send.at[kind],
            recv_sem=end_recv.at[kind],
            device_id=tensor_peer[peer],
            device_id_type=MESH,
        )

    ends = (
        end_copy(half_out, half_in, 0, "mate"),
        end_copy(sum_out, sum_in, 1, "far"),
        end_copy(full_in.at[core], full_in.at[core], 2, "mate"),
    )
    ends[0].start()
    ends[0].wait_recv()
    pair_sum = out_sum[:, side(core)] + half_in[...].astype(jnp.float32)
    sum_out[...] = pair_sum.astype(jnp.bfloat16)
    ends[1].start()
    ends[1].wait_recv()
    full_in[core] = (pair_sum + sum_in[...].astype(jnp.float32)).astype(jnp.bfloat16)
    ends[2].start()
    end_copy(full_in.at[core], full_in.at[1 - core], 2, "mate").wait_recv()
    total = jnp.concatenate([full_in[0], full_in[1]], axis=1).astype(jnp.float32)
    decoded[...] = normalize(decoder_in[...].astype(jnp.float32) + total).astype(jnp.bfloat16)

    for h in range(parts):
        for s in range(experts):
            b = order[s]

            @pl.when((b <= e) & (e + 1 < experts))
            def _():
                line(b, True, h).wait_send()

            @pl.when((b >= e) & (e > 0))
            def _():
                line(b, False, h).wait_send()

            if s > 0:
                spread(b, t, h, 0, "far").wait_send()
                spread(b, t, h, 1, "mate").wait_send()
                spread(b, far, h, 2, "mate").wait_send()
    for k in range(per):
        for s in range(experts):
            pair_copy(s, k).wait_send()
            chip_copy(s, k).wait_send()
            if s > 0:
                back_copy(s, k).wait_send()
        gather(t, k, 0, "far").wait_send()
        gather(t, k, 1, "mate").wait_send()
        gather(far, k, 2, "mate").wait_send()
    for end in ends:
        end.wait_send()


def dense_shards(
    source_states,
    routes,
    router_weight,
    fc1_weight,
    fc2_weight,
    lengths,
    lang_ids,
    pivot_states,
    query_weight,
    key_weight,
    value_weight,
    out_weight,
):
    tok_count, model_width = source_states.shape
    experts = router_weight.shape[1]
    tensor_count = lax.axis_size("tensor")
    chips = tensor_count // 2
    columns = model_width // tensor_count
    row_count = lengths.shape[1] * pivot_states.shape[0]
    per = columns // TILE
    parts = 2
    vmem = pl.BlockSpec(memory_space=pltpu.VMEM)
    hbm = pl.BlockSpec(memory_space=pl.ANY)
    bf16, f32, dma = jnp.bfloat16, jnp.float32, pltpu.SemaphoreType.DMA
    units = fc1_weight.shape[2]
    half = model_width // 2
    return pl.pallas_call(
        functools.partial(layer_kernel, experts, chips),
        out_shape=(
            jax.ShapeDtypeStruct((tok_count, columns), bf16),
            jax.ShapeDtypeStruct((row_count, model_width), bf16),
        ),
        in_specs=[vmem] * 6 + [hbm] * 6,
        out_specs=(vmem, vmem),
        scratch_shapes=[
            pltpu.VMEM((model_width, units), bf16),
            pltpu.VMEM((units, model_width), bf16),
            pltpu.VMEM((model_width, columns), bf16),
            pltpu.VMEM((model_width, columns), bf16),
            pltpu.VMEM((model_width, columns), bf16),
            pltpu.VMEM((columns, model_width), bf16),
            pltpu.VMEM((tok_count, experts), f32),
            pltpu.VMEM((row_count, model_width), bf16),
            pltpu.VMEM((row_count, columns), bf16),
            pltpu.VMEM((experts, tok_count, model_width), bf16),
            pltpu.VMEM((tok_count, units), bf16),
            pltpu.VMEM((experts, per, chips, tok_count, TILE), bf16),
            pltpu.VMEM((experts, per, chips, tok_count, TILE), bf16),
            pltpu.VMEM((experts, per, chips, tok_count, TILE), f32),
            pltpu.VMEM((experts, per, tok_count, TILE), bf16),
            pltpu.VMEM((experts, per, tok_count, TILE), bf16),
            pltpu.VMEM((experts, per, tok_count, TILE), bf16),
            pltpu.VMEM((experts, per, tok_count, TILE), bf16),
            pltpu.VMEM((tok_count, model_width), bf16),
            pltpu.VMEM((tok_count, columns), f32),
            pltpu.VMEM((tok_count, columns), f32),
            pltpu.VMEM((row_count, columns), bf16),
            pltpu.VMEM((row_count, model_width), f32),
            pltpu.VMEM((row_count, half), bf16),
            pltpu.VMEM((row_count, half), bf16),
            pltpu.VMEM((row_count, half), bf16),
            pltpu.VMEM((row_count, half), bf16),
            pltpu.VMEM((2, row_count, half), bf16),
            dma((6,)),
            dma((experts, parts)),
            dma((experts, parts)),
            dma((experts, parts)),
            dma((3, experts, parts)),
            dma((3, experts, parts)),
            dma((3, experts, per)),
            dma((3, experts, per)),
            dma((3, per)),
            dma((3, per)),
            dma((3,)),
            dma((3,)),
        ],
        compiler_params=pltpu.CompilerParams(
            collective_id=0, has_side_effects=True, vmem_limit_bytes=60 * 2**20
        ),
    )(
        source_states,
        routes,
        router_weight,
        lengths,
        lang_ids,
        pivot_states,
        fc1_weight[0],
        fc2_weight[0],
        query_weight,
        key_weight,
        value_weight,
        out_weight,
    )


def solution(mesh):
    in_specs = (
        P(("groups", "expert"), None),
        P(("groups", "expert"), None),
        P(),
        P("expert", None, "tensor"),
        P("expert", "tensor", None),
        P(("groups", "expert"), None),
        P(("groups", "expert"), None),
        P(),
        P(None, "tensor"),
        P(None, "tensor"),
        P(None, "tensor"),
        P("tensor", None),
    )
    out_specs = (P(("groups", "expert"), "tensor"), P(("groups", "expert"), None))
    sizes = dict(mesh.shape)
    shards = dense_shards if sizes["expert"] == 4 and sizes["tensor"] == 4 else packed_shards
    return jax.shard_map(shards, mesh=mesh, in_specs=in_specs, out_specs=out_specs, check_vma=False)
```

```python
import functools

import jax
import jax.numpy as jnp
from jax import lax
from jax.experimental import pallas as pl
from jax.experimental.pallas import tpu as pltpu
from jax.sharding import PartitionSpec as P

HD = 128


EPSILON = 1e-05
NEGATIVE = -1e30


def normalize(values):
    values = values.astype(jnp.float32)
    center = jnp.mean(values, axis=-1, keepdims=True)
    shifted = values - center
    spread = jnp.mean(shifted * shifted, axis=-1, keepdims=True)
    return shifted * lax.rsqrt(spread + EPSILON)


def route_tables(routes, experts, capacity):
    tok_count = routes.shape[0]
    expert_iota = jnp.arange(experts, dtype=jnp.int32)
    chosen = routes[:, :, None] == expert_iota[None, None, :]
    flat_chosen = chosen.reshape(tok_count * 2, experts).astype(jnp.bfloat16)
    pair_iota = jnp.arange(tok_count * 2, dtype=jnp.int32)
    earlier = (pair_iota[None, :] < pair_iota[:, None]).astype(jnp.bfloat16)
    before = jnp.dot(earlier, flat_chosen, preferred_element_type=jnp.float32)
    slots = jnp.sum(before * flat_chosen.astype(jnp.float32), axis=1)
    slots = slots.astype(jnp.int32).reshape(tok_count, 2)
    slot_iota = jnp.arange(capacity, dtype=jnp.int32)
    placed = chosen[:, :, :, None] & (slots[:, :, None, None] == slot_iota[None, None, None, :])
    return (chosen, placed.reshape(tok_count, 2, experts * capacity).astype(jnp.bfloat16))


def project_pair(key_weight, value_weight):

    def project(totals, shard_part, offset):
        return (
            jnp.dot(shard_part, key_weight, preferred_element_type=jnp.float32),
            jnp.dot(shard_part, value_weight, preferred_element_type=jnp.float32),
        )

    return project


def packed_shards(
    source_states,
    routes,
    router_weight,
    fc1_weight,
    fc2_weight,
    lengths,
    lang_ids,
    pivot_states,
    query_weight,
    key_weight,
    value_weight,
    out_weight,
):
    tok_count, model_width = source_states.shape
    experts = router_weight.shape[1]
    capacity = 4 * tok_count // experts
    tensor_count = lax.axis_size("tensor")
    column_width = model_width // tensor_count
    column_start = lax.axis_index("tensor") * column_width
    normed = normalize(source_states).astype(jnp.bfloat16)
    logits = jnp.dot(normed, router_weight, preferred_element_type=jnp.float32)
    chosen, placed = route_tables(routes, experts, capacity)
    pair_logits = jnp.sum(jnp.where(chosen, logits[:, None, :], 0.0), axis=2)
    gate_values = jax.nn.sigmoid(pair_logits - pair_logits[:, ::-1])
    occupied = jnp.sum(placed, axis=1)
    outgoing = jnp.einsum("ts,td->sd", occupied, normed, preferred_element_type=jnp.float32)
    outgoing = outgoing.astype(jnp.bfloat16).reshape(experts, capacity, model_width)
    weight_in = fc1_weight[0]
    weight_back = fc2_weight[0]
    arrived = lax.all_to_all(outgoing, "expert", split_axis=0, concat_axis=0, tiled=True)
    row_block = arrived.reshape(-1, model_width)
    hidden = jnp.maximum(
        jnp.dot(row_block, weight_in, preferred_element_type=jnp.float32), 0.0
    ).astype(jnp.bfloat16)
    partial_value = jnp.dot(hidden, weight_back, preferred_element_type=jnp.float32).astype(
        jnp.bfloat16
    )
    partials = partial_value.reshape(arrived.shape)
    zeroed = jnp.zeros((tok_count, key_weight.shape[1]), jnp.float32)
    project = project_pair(key_weight, value_weight)
    own_cols = lax.dynamic_slice_in_dim(source_states, column_start, column_width, 1).astype(
        jnp.float32
    )
    widened = partials.astype(jnp.float32)
    summed = lax.psum_scatter(
        widened.astype(jnp.bfloat16), "tensor", scatter_dimension=2, tiled=True
    )
    returned_rows = lax.all_to_all(summed, "expert", split_axis=0, concat_axis=0, tiled=True)
    picked = jnp.einsum(
        "tks,sd->tkd",
        placed,
        returned_rows.reshape(experts * capacity, column_width),
        preferred_element_type=jnp.float32,
    )
    encoded = (own_cols + jnp.sum(gate_values[:, :, None] * picked, axis=1)).astype(jnp.bfloat16)
    key_sum, value_sum = project(
        (zeroed, zeroed), lax.all_gather(encoded, "tensor", axis=1, tiled=True), jnp.int32(0)
    )
    key_cache = key_sum.astype(jnp.bfloat16)
    value_cache = value_sum.astype(jnp.bfloat16)
    query_count = lengths.shape[1]
    pivot_count = pivot_states.shape[0]
    row_count = query_count * pivot_count
    query_iota = jnp.arange(query_count, dtype=jnp.int32)
    query_ends = jnp.sum(
        jnp.where(query_iota[None, :] <= query_iota[:, None], lengths[0][None, :], 0), axis=1
    )
    positions = jnp.arange(tok_count, dtype=jnp.int32)
    key_owner = jnp.sum((positions[:, None] >= query_ends[None, :]).astype(jnp.int32), axis=1)
    row_owner = jnp.arange(row_count, dtype=jnp.int32) // pivot_count
    allowed = row_owner[:, None] == key_owner[None, :]
    language_pick = (
        lang_ids.reshape(-1)[:, None] == jnp.arange(pivot_count, dtype=jnp.int32)[None, :]
    ).astype(jnp.bfloat16)
    decoder_in = jnp.dot(language_pick, pivot_states, preferred_element_type=jnp.float32).astype(
        jnp.bfloat16
    )
    queries = jnp.dot(decoder_in, query_weight, preferred_element_type=jnp.float32).astype(
        jnp.bfloat16
    )
    head_local = queries.shape[1] // HD
    query_heads = queries.reshape(row_count, head_local, HD)
    key_heads = key_cache.reshape(tok_count, head_local, HD)
    value_heads = value_cache.reshape(tok_count, head_local, HD)
    scores = jnp.einsum(
        "rhe,the->hrt", query_heads, key_heads, preferred_element_type=jnp.float32
    ) * HD ** (-0.5)
    scores = jnp.where(allowed[None], scores, NEGATIVE)
    row_max = jnp.max(scores, axis=2, keepdims=True)
    weights = jnp.exp(scores - row_max)
    attention = (weights / jnp.sum(weights, axis=2, keepdims=True)).astype(jnp.bfloat16)
    context = jnp.einsum(
        "hrt,the->rhe", attention, value_heads, preferred_element_type=jnp.float32
    ).astype(jnp.bfloat16)
    partial_out = jnp.dot(
        context.reshape(row_count, head_local * HD), out_weight, preferred_element_type=jnp.float32
    )
    attn_total = lax.psum(partial_out.astype(jnp.bfloat16), "tensor").astype(jnp.float32)
    decoded = normalize(decoder_in.astype(jnp.float32) + attn_total).astype(jnp.bfloat16)
    return (encoded, decoded)


MESH = pl.DeviceIdType.MESH
TILE = 256


def layer_kernel(
    experts,
    chips,
    source,
    routes,
    router_w,
    lengths,
    languages,
    pivots,
    fc1_hbm,
    fc2_hbm,
    query_hbm,
    key_hbm,
    value_hbm,
    out_hbm,
    encoded,
    decoded,
    fc1,
    fc2,
    query_w,
    key_w,
    value_w,
    out_w,
    gates,
    decoder_in,
    queries,
    rows,
    hidden,
    core_out,
    core_in,
    kept,
    chip_out,
    chip_in,
    back_out,
    back_in,
    gathered,
    key_sum,
    value_sum,
    context,
    out_sum,
    half_out,
    half_in,
    sum_out,
    sum_in,
    full_in,
    load_sem,
    up_sem,
    down_sem,
    line_recv,
    send_sem,
    recv_sem,
    ret_send,
    ret_recv,
    gat_send,
    gat_recv,
    end_send,
    end_recv,
):
    tokens, width = source.shape
    columns = encoded.shape[1]
    parts = 2
    part_rows = tokens // parts
    per = columns // TILE
    e = lax.axis_index("expert")
    t = lax.axis_index("tensor")
    chip, core = t // 2, t % 2
    mate = chip * 2 + 1 - core
    far = (1 - chip) * 2 + core
    far_mate = (1 - chip) * 2 + 1 - core
    tensor_peer = {"mate": {"tensor": mate}, "far": {"tensor": far}}

    def same(i):
        return 1 - ((e - i + experts) % experts + experts - 1) // experts

    nearest = [
        sorted(range(experts), key=lambda b, i=i: (abs(b - i), abs(2 * b - experts + 1)))
        for i in range(experts)
    ]
    order = [sum(same(i) * nearest[i][s] for i in range(experts)) for s in range(experts)]

    loads = [
        pltpu.make_async_copy(src, dst, load_sem.at[i])
        for i, (src, dst) in enumerate(
            (
                (fc1_hbm, fc1),
                (fc2_hbm, fc2),
                (query_hbm, query_w),
                (key_hbm, key_w),
                (value_hbm, value_w),
                (out_hbm, out_w),
            )
        )
    ]
    for load in loads:
        load.start()

    barrier = pltpu.get_barrier_semaphore()
    for step in range(1, experts):
        pl.semaphore_signal(
            barrier, 1, device_id={"expert": (e + step) % experts}, device_id_type=MESH
        )
    for peer in tensor_peer.values():
        pl.semaphore_signal(barrier, 1, device_id=peer, device_id_type=MESH)

    def quarter(q):
        return pl.ds(pl.multiple_of(q * columns, columns), columns)

    rows[e] = normalize(source[...]).astype(jnp.bfloat16)
    pl.semaphore_wait(barrier, experts + 1)

    def line(b, up, h):
        piece = rows.at[b, pl.ds(h * part_rows, part_rows), quarter(t)]
        return pltpu.make_async_remote_copy(
            src_ref=piece,
            dst_ref=piece,
            send_sem=(up_sem if up else down_sem).at[b, h],
            recv_sem=line_recv.at[b, h],
            device_id={"expert": (e + 1) % experts if up else (e + experts - 1) % experts},
            device_id_type=MESH,
        )

    def spread(b, q, h, kind, peer):
        piece = rows.at[b, pl.ds(h * part_rows, part_rows), quarter(q)]
        return pltpu.make_async_remote_copy(
            src_ref=piece,
            dst_ref=piece,
            send_sem=send_sem.at[kind, b, h],
            recv_sem=recv_sem.at[kind, b, h],
            device_id=tensor_peer[peer],
            device_id_type=MESH,
        )

    @pl.when(e + 1 < experts)
    def _():
        for h in range(parts):
            line(e, True, h).start()

    @pl.when(e > 0)
    def _():
        for h in range(parts):
            line(e, False, h).start()

    def arrive(s, h):
        b = order[s]
        line(b, True, h).wait_recv()

        @pl.when((b < e) & (e + 1 < experts))
        def _():
            line(b, True, h).start()

        @pl.when((b > e) & (e > 0))
        def _():
            line(b, False, h).start()

        spread(b, t, h, 0, "far").start()
        spread(b, t, h, 1, "mate").start()

    def relay(s, h):
        b = order[s]
        spread(b, far, h, 0, "far").wait_recv()
        spread(b, far, h, 2, "mate").start()

    def ready(s):
        b = order[s]
        for h in range(parts):
            spread(b, mate, h, 1, "mate").wait_recv()
            spread(b, far_mate, h, 2, "mate").wait_recv()

    tiles = hidden.shape[1] // TILE

    def first(s, a):
        b = order[s]

        @pl.loop(a * (tiles // 2), (a + 1) * (tiles // 2))
        def _(j):
            at = pl.ds(pl.multiple_of(j * TILE, TILE), TILE)
            tile = jnp.dot(rows[b], fc1[:, at], preferred_element_type=jnp.float32)
            hidden[:, at] = jnp.maximum(tile, 0.0).astype(jnp.bfloat16)

    def second_tile(p, c, k):
        at = pl.ds(pl.multiple_of((p * 2 + c) * columns + k * TILE, TILE), TILE)
        return jnp.dot(hidden[...], fc2[:, at], preferred_element_type=jnp.float32)

    def second(s, k):
        @pl.loop(0, chips)
        def _(p):
            core_out[s, k, p] = second_tile(p, 1 - core, k).astype(jnp.bfloat16)

        pair_copy(s, k).start()

        @pl.loop(0, chips)
        def _(p):
            kept[s, k, p] = second_tile(p, core, k)

    def pair_copy(s, k):
        return pltpu.make_async_remote_copy(
            src_ref=core_out.at[s, k],
            dst_ref=core_in.at[s, k],
            send_sem=ret_send.at[0, s, k],
            recv_sem=ret_recv.at[0, s, k],
            device_id=tensor_peer["mate"],
            device_id_type=MESH,
        )

    def chip_copy(s, k):
        return pltpu.make_async_remote_copy(
            src_ref=chip_out.at[s, k],
            dst_ref=chip_in.at[s, k],
            send_sem=ret_send.at[1, s, k],
            recv_sem=ret_recv.at[1, s, k],
            device_id=tensor_peer["far"],
            device_id_type=MESH,
        )

    def back_copy(s, k):
        return pltpu.make_async_remote_copy(
            src_ref=back_out.at[s, k],
            dst_ref=back_in.at[e, k],
            send_sem=ret_send.at[2, s, k],
            recv_sem=ret_recv.at[2, e, k],
            device_id={"expert": order[s]},
            device_id_type=MESH,
        )

    def back_wait(i, k):
        return pltpu.make_async_remote_copy(
            src_ref=back_out.at[0, k],
            dst_ref=back_in.at[i, k],
            send_sem=ret_send.at[2, 0, k],
            recv_sem=ret_recv.at[2, i, k],
            device_id={"expert": i},
            device_id_type=MESH,
        )

    def reduce_pair(s, k):
        pair_copy(s, k).wait_recv()
        other = 1 - chip
        chip_out[s, k] = (
            kept[s, k, other] + core_in[s, k, other].astype(jnp.float32)
        ).astype(jnp.bfloat16)
        chip_copy(s, k).start()

    def reduce_chips(s, k):
        chip_copy(s, k).wait_recv()
        total = (
            kept[s, k, chip]
            + core_in[s, k, chip].astype(jnp.float32)
            + chip_in[s, k].astype(jnp.float32)
        ).astype(jnp.bfloat16)
        if s == 0:
            back_in[e, k] = total
        else:
            back_out[s, k] = total
            back_copy(s, k).start()

    def route():
        logits = lax.dot_general(
            router_w[...],
            rows[e],
            (((1,), (1,)), ((), ())),
            preferred_element_type=jnp.float32,
        )
        place = lax.broadcasted_iota(jnp.int32, logits.shape, 0)
        chosen = [routes[i : i + 1, :] == place for i in range(2)]
        picked = [jnp.sum(jnp.where(c, logits, 0.0), axis=0, keepdims=True) for c in chosen]
        difference = picked[0] - picked[1]
        table = jnp.where(chosen[0], jax.nn.sigmoid(difference), 0.0) + jnp.where(
            chosen[1], jax.nn.sigmoid(-difference), 0.0
        )
        gates[...] = jnp.transpose(table)

    query_count, pivot_count = languages.shape
    row_count = decoded.shape[0]

    def ask():
        place = lax.broadcasted_iota(jnp.int32, (row_count, query_count), 0)
        query = lax.broadcasted_iota(jnp.int32, (row_count, query_count), 1)
        below, above = query * pivot_count, (query + 1) * pivot_count
        owner = ((place >= below) & (place < above)).astype(jnp.float32)
        named = jnp.dot(
            owner, languages[...].astype(jnp.float32), preferred_element_type=jnp.float32
        )
        first_row = jnp.zeros((row_count, pivot_count), jnp.int32)
        place = lax.broadcasted_iota(jnp.int32, (row_count, pivot_count), 0)
        for i in range(1, query_count):
            first_row = first_row + jnp.where(place >= i * pivot_count, pivot_count, 0)
        lane = lax.broadcasted_iota(jnp.int32, (row_count, pivot_count), 1)
        language = jnp.sum(
            jnp.where(place - first_row == lane, named, 0.0), axis=1, keepdims=True
        )
        pick = (jnp.abs(language - lane.astype(jnp.float32)) < 0.5).astype(jnp.bfloat16)
        decoder_in[...] = jnp.dot(
            pick, pivots[...], preferred_element_type=jnp.float32
        ).astype(jnp.bfloat16)
        loads[2].wait()
        queries[...] = jnp.dot(
            decoder_in[...], query_w[...], preferred_element_type=jnp.float32
        ).astype(jnp.bfloat16)

    loads[0].wait()
    first(0, 0)
    arrive(1, 0)
    first(0, 1)
    arrive(1, 1)
    loads[1].wait()
    second(0, 0)
    relay(1, 0)
    second(0, 1)
    relay(1, 1)
    arrive(2, 0)
    ask()
    arrive(2, 1)
    route()
    ready(1)
    first(1, 0)
    arrive(3, 0)
    relay(2, 0)
    first(1, 1)
    arrive(3, 1)
    relay(2, 1)
    second(1, 0)
    relay(3, 0)
    reduce_pair(1, 0)
    second(1, 1)
    relay(3, 1)
    reduce_pair(1, 1)
    ready(2)
    first(2, 0)
    first(2, 1)
    second(2, 0)
    reduce_pair(2, 0)
    second(2, 1)
    reduce_pair(2, 1)
    ready(3)
    first(3, 0)
    reduce_chips(1, 0)
    first(3, 1)
    reduce_chips(1, 1)
    second(3, 0)
    reduce_pair(3, 0)
    second(3, 1)
    reduce_pair(3, 1)
    reduce_pair(0, 0)
    reduce_pair(0, 1)
    reduce_chips(2, 0)
    reduce_chips(2, 1)
    reduce_chips(3, 0)
    reduce_chips(3, 1)

    def part(q, k):
        return pl.ds(pl.multiple_of(q * columns + k * TILE, TILE), TILE)

    def gather(q, k, kind, peer):
        piece = gathered.at[:, part(q, k)]
        return pltpu.make_async_remote_copy(
            src_ref=piece,
            dst_ref=piece,
            send_sem=gat_send.at[kind, k],
            recv_sem=gat_recv.at[kind, k],
            device_id=tensor_peer[peer],
            device_id_type=MESH,
        )

    def project(q, k, fresh):
        piece = gathered[:, part(q, k)]
        for weight, total in ((key_w, key_sum), (value_w, value_sum)):
            term = jnp.dot(piece, weight[part(q, k), :], preferred_element_type=jnp.float32)
            total[...] = term if fresh else total[...] + term

    for load in loads[3:]:
        load.wait()
    for k in range(per):
        reduce_chips(0, k)
        for s in range(1, experts):
            back_wait(order[s], k).wait_recv()
        mixed = source[:, part(t, k)].astype(jnp.float32)
        for i in range(experts):
            mixed = mixed + gates[:, i : i + 1] * back_in[i, k].astype(jnp.float32)
        mixed = mixed.astype(jnp.bfloat16)
        gathered[:, part(t, k)] = mixed
        gather(t, k, 0, "far").start()
        gather(t, k, 1, "mate").start()
        encoded[:, k * TILE : (k + 1) * TILE] = mixed
        project(t, k, k == 0)
    for k in range(per):
        gather(mate, k, 1, "mate").wait_recv()
        gather(far, k, 0, "far").wait_recv()
        gather(far, k, 2, "mate").start()
        project(mate, k, False)
        project(far, k, False)
    for k in range(per):
        gather(far_mate, k, 2, "mate").wait_recv()
        project(far_mate, k, False)

    position = lax.broadcasted_iota(jnp.int32, (row_count, tokens), 1)
    place = lax.broadcasted_iota(jnp.int32, (row_count, tokens), 0)
    end = jnp.zeros((1, 1), jnp.int32)
    allowed = jnp.zeros((row_count, tokens), jnp.float32)
    for i in range(query_count):
        begin, end = end, end + lengths[:, i : i + 1]
        inside = (position >= begin) & (position < end)
        inside = inside & (place >= i * pivot_count) & (place < (i + 1) * pivot_count)
        allowed = jnp.where(inside, 1.0, allowed)

    for h in range(columns // HD):
        at = slice(h * HD, (h + 1) * HD)
        scores = lax.dot_general(
            queries[:, at],
            key_sum[:, at].astype(jnp.bfloat16),
            (((1,), (1,)), ((), ())),
            preferred_element_type=jnp.float32,
        ) * HD ** (-0.5)
        scores = jnp.where(allowed > 0.5, scores, NEGATIVE)
        weights = jnp.exp(scores - jnp.max(scores, axis=1, keepdims=True))
        attention = (weights / jnp.sum(weights, axis=1, keepdims=True)).astype(jnp.bfloat16)
        context[:, at] = jnp.dot(
            attention, value_sum[:, at].astype(jnp.bfloat16), preferred_element_type=jnp.float32
        ).astype(jnp.bfloat16)

    half = width // 2

    def side(c):
        return pl.ds(pl.multiple_of(c * half, half), half)

    out_sum[...] = jnp.dot(context[...], out_w[...], preferred_element_type=jnp.float32)
    half_out[...] = out_sum[:, side(1 - core)].astype(jnp.bfloat16)

    def end_copy(src, dst, kind, peer):
        return pltpu.make_async_remote_copy(
            src_ref=src,
            dst_ref=dst,
            send_sem=end_send.at[kind],
            recv_sem=end_recv.at[kind],
            device_id=tensor_peer[peer],
            device_id_type=MESH,
        )

    ends = (
        end_copy(half_out, half_in, 0, "mate"),
        end_copy(sum_out, sum_in, 1, "far"),
        end_copy(full_in.at[core], full_in.at[core], 2, "mate"),
    )
    ends[0].start()
    ends[0].wait_recv()
    pair_sum = out_sum[:, side(core)] + half_in[...].astype(jnp.float32)
    sum_out[...] = pair_sum.astype(jnp.bfloat16)
    ends[1].start()
    ends[1].wait_recv()
    full_in[core] = (pair_sum + sum_in[...].astype(jnp.float32)).astype(jnp.bfloat16)
    ends[2].start()
    end_copy(full_in.at[core], full_in.at[1 - core], 2, "mate").wait_recv()
    total = jnp.concatenate([full_in[0], full_in[1]], axis=1).astype(jnp.float32)
    decoded[...] = normalize(decoder_in[...].astype(jnp.float32) + total).astype(jnp.bfloat16)

    for h in range(parts):
        for s in range(experts):
            b = order[s]

            @pl.when((b <= e) & (e + 1 < experts))
            def _():
                line(b, True, h).wait_send()

            @pl.when((b >= e) & (e > 0))
            def _():
                line(b, False, h).wait_send()

            if s > 0:
                spread(b, t, h, 0, "far").wait_send()
                spread(b, t, h, 1, "mate").wait_send()
                spread(b, far, h, 2, "mate").wait_send()
    for k in range(per):
        for s in range(experts):
            pair_copy(s, k).wait_send()
            chip_copy(s, k).wait_send()
            if s > 0:
                back_copy(s, k).wait_send()
        gather(t, k, 0, "far").wait_send()
        gather(t, k, 1, "mate").wait_send()
        gather(far, k, 2, "mate").wait_send()
    for end in ends:
        end.wait_send()


def dense_shards(
    source_states,
    routes,
    router_weight,
    fc1_weight,
    fc2_weight,
    lengths,
    lang_ids,
    pivot_states,
    query_weight,
    key_weight,
    value_weight,
    out_weight,
):
    tok_count, model_width = source_states.shape
    experts = router_weight.shape[1]
    tensor_count = lax.axis_size("tensor")
    chips = tensor_count // 2
    columns = model_width // tensor_count
    row_count = lengths.shape[1] * pivot_states.shape[0]
    per = columns // TILE
    parts = 2
    vmem = pl.BlockSpec(memory_space=pltpu.VMEM)
    hbm = pl.BlockSpec(memory_space=pl.ANY)
    bf16, f32, dma = jnp.bfloat16, jnp.float32, pltpu.SemaphoreType.DMA
    units = fc1_weight.shape[2]
    half = model_width // 2
    return pl.pallas_call(
        functools.partial(layer_kernel, experts, chips),
        out_shape=(
            jax.ShapeDtypeStruct((tok_count, columns), bf16),
            jax.ShapeDtypeStruct((row_count, model_width), bf16),
        ),
        in_specs=[vmem] * 6 + [hbm] * 6,
        out_specs=(vmem, vmem),
        scratch_shapes=[
            pltpu.VMEM((model_width, units), bf16),
            pltpu.VMEM((units, model_width), bf16),
            pltpu.VMEM((model_width, columns), bf16),
            pltpu.VMEM((model_width, columns), bf16),
            pltpu.VMEM((model_width, columns), bf16),
            pltpu.VMEM((columns, model_width), bf16),
            pltpu.VMEM((tok_count, experts), f32),
            pltpu.VMEM((row_count, model_width), bf16),
            pltpu.VMEM((row_count, columns), bf16),
            pltpu.VMEM((experts, tok_count, model_width), bf16),
            pltpu.VMEM((tok_count, units), bf16),
            pltpu.VMEM((experts, per, chips, tok_count, TILE), bf16),
            pltpu.VMEM((experts, per, chips, tok_count, TILE), bf16),
            pltpu.VMEM((experts, per, chips, tok_count, TILE), f32),
            pltpu.VMEM((experts, per, tok_count, TILE), bf16),
            pltpu.VMEM((experts, per, tok_count, TILE), bf16),
            pltpu.VMEM((experts, per, tok_count, TILE), bf16),
            pltpu.VMEM((experts, per, tok_count, TILE), bf16),
            pltpu.VMEM((tok_count, model_width), bf16),
            pltpu.VMEM((tok_count, columns), f32),
            pltpu.VMEM((tok_count, columns), f32),
            pltpu.VMEM((row_count, columns), bf16),
            pltpu.VMEM((row_count, model_width), f32),
            pltpu.VMEM((row_count, half), bf16),
            pltpu.VMEM((row_count, half), bf16),
            pltpu.VMEM((row_count, half), bf16),
            pltpu.VMEM((row_count, half), bf16),
            pltpu.VMEM((2, row_count, half), bf16),
            dma((6,)),
            dma((experts, parts)),
            dma((experts, parts)),
            dma((experts, parts)),
            dma((3, experts, parts)),
            dma((3, experts, parts)),
            dma((3, experts, per)),
            dma((3, experts, per)),
            dma((3, per)),
            dma((3, per)),
            dma((3,)),
            dma((3,)),
        ],
        compiler_params=pltpu.CompilerParams(
            collective_id=0, has_side_effects=True, vmem_limit_bytes=60 * 2**20
        ),
    )(
        source_states,
        routes.T,
        router_weight.T,
        lengths,
        lang_ids,
        pivot_states,
        fc1_weight[0],
        fc2_weight[0],
        query_weight,
        key_weight,
        value_weight,
        out_weight,
    )


def solution(mesh):
    in_specs = (
        P(("groups", "expert"), None),
        P(("groups", "expert"), None),
        P(),
        P("expert", None, "tensor"),
        P("expert", "tensor", None),
        P(("groups", "expert"), None),
        P(("groups", "expert"), None),
        P(),
        P(None, "tensor"),
        P(None, "tensor"),
        P(None, "tensor"),
        P("tensor", None),
    )
    out_specs = (P(("groups", "expert"), "tensor"), P(("groups", "expert"), None))
    sizes = dict(mesh.shape)
    shards = dense_shards if sizes["expert"] == 4 and sizes["tensor"] == 4 else packed_shards
    return jax.shard_map(shards, mesh=mesh, in_specs=in_specs, out_specs=out_specs, check_vma=False)
```
